32 devices in a mesh: row: 8 (over z, y), col: 4 (over x, core).
Axes of the slice: x: 2, y: 2, z: 4, core: 2. Of those that a mesh axis runs over, the one named last changes fastest.
Arguments:
- diag_block: float32 [2048, 2048], P('row'), as said below
- z_panel: float32 [2048, 2048], P('row', 'col'), may hold values from -0.046875 to 0.046875
- panel_below: float32 [16384, 2048], P('row', 'col'), may hold values from -6 to 6
- z_trail: float32 [16384, 2048], P('row', 'col'), may hold values from -6 to 6
- norm_sq: float32 [2048], P('col'), may hold values from 0.05 to 0.5
Outputs:
- norm_out: float32 [2048], P('col')
- trail_out: float32 [16384, 2048], P('row', 'col')
The draws below stay inside these ranges and needn't reach their ends.
Inputs may be any that keep to these rules, and one draw needn't show every extreme that they name: diag_block is zero above its diagonal; its diagonal entries are at least 1.
All inputs are finite; a program needn't handle non-finite values.
Results may differ from the reference program's by a relative error of at most 0.00017.
Values sent between devices are 32-bit elements; how exact they have to be, the bound alone decides.
No kernel may reach another device: no remote copies, remote signals or barrier semaphores. Data moves between devices by JAX's collectives and lax.ppermute only.
A program may use at most 64 MiB of HBM per device.

```python
import math
import jax
import jax.numpy as jnp
from jax import lax

NB = 2048
OBS = 2048
TRAIL = 16384


def draw_diag_block(key, part):
    key_lower, key_pivot = jax.random.split(jax.random.fold_in(key, 11))
    rows = lax.broadcasted_iota(jnp.int32, (NB, NB), 0)
    cols = lax.broadcasted_iota(jnp.int32, (NB, NB), 1)
    lower = jax.random.normal(key_lower, (NB, NB), jnp.float32) * (4.0 / math.sqrt(NB))
    pivots = jax.random.uniform(key_pivot, (NB, NB), jnp.float32, 1.0, 2.0)
    return jnp.where(rows > cols, lower, jnp.where(rows == cols, pivots, 0.0)).astype(jnp.float32)


def shard_levels(stream_key, extent, cuts, smallest, high):
    loudness = 1.0
    for position, blocks in cuts:
        draws = jax.random.uniform(jax.random.fold_in(jax.random.fold_in(stream_key, 6), position), (blocks,), jnp.float32, smallest / len(cuts), high / len(cuts))
        loudness = loudness * jnp.repeat(jnp.exp(draws), extent[position] // blocks).reshape((-1,) + (1,) * (len(extent) - 1 - position))
    return loudness


def bell_draw(key, extent, width, most, cuts=(), kind=jnp.bfloat16):
    gain = shard_levels(key, extent, cuts, -0.22, 0.18) if cuts else 1.0
    result = jax.random.normal(key, extent, jnp.float32) * width * gain
    return jnp.minimum(jnp.maximum(result, -most), most).astype(kind)


def setup_inputs(seed: int = 0) -> dict:
    arg_keys = jax.random.split(jax.random.key(seed), 6)
    diag_block = draw_diag_block(jax.random.fold_in(arg_keys[5], 71), 0)
    z_panel = bell_draw(arg_keys[1], (NB, OBS), (8 * NB) ** -0.5, 0.046875, ((0, 8), (1, 4)), jnp.float32)
    panel_below = bell_draw(arg_keys[2], (TRAIL, NB), 1.0, 6.0, ((0, 8), (1, 4)), jnp.float32)
    z_trail = bell_draw(arg_keys[3], (TRAIL, OBS), 1.0, 6.0, ((0, 8), (1, 4)), jnp.float32)
    norm_sq = jnp.clip(0.05 + 0.45 * jax.random.uniform(arg_keys[4], (OBS,), jnp.float32) ** shard_levels(arg_keys[4], (OBS,), ((0, 4),), -0.2, 0.2), 0.05, 0.5)
    return {"diag_block": diag_block, "z_panel": z_panel, "panel_below": panel_below, "z_trail": z_trail, "norm_sq": norm_sq}


def reference(diag_block, z_panel, panel_below, z_trail, norm_sq):
    solved = lax.linalg.triangular_solve(diag_block, z_panel, left_side=True, lower=True)
    norm_out = norm_sq + jnp.sum(solved * solved, axis=0)
    update = jnp.dot(panel_below.astype(jnp.float32), solved.astype(jnp.float32), precision=lax.Precision.HIGHEST, preferred_element_type=jnp.float32)
    trail_out = z_trail - update
    return (norm_out, trail_out)
```

```python
import jax
import jax.numpy as jnp
from jax import lax
from jax.experimental import pallas as pl
from jax.experimental.pallas import tpu as pltpu
from jax.sharding import PartitionSpec as P

F32 = jnp.float32
BF16 = jnp.bfloat16
HIGHEST = lax.Precision.HIGHEST
CHUNKS = 2
ROW_PIECES = (4, 4, 4, 2, 2)
ANY = pl.BlockSpec(memory_space=pl.ANY)
VMEM = pl.BlockSpec(memory_space=pltpu.VMEM)
LIMIT = 48 * 1024 * 1024


def params(**more):
    return pltpu.CompilerParams(vmem_limit_bytes=LIMIT, **more)


def mul(a, b):
    return jnp.dot(a, b, precision=HIGHEST, preferred_element_type=F32)


def mul_t(a, b):
    return lax.dot_general(
        a, b, (((1,), (1,)), ((), ())), precision=HIGHEST, preferred_element_type=F32
    )


def level_and_half():
    own_row = lax.axis_index("row")
    return own_row // 2, own_row % 2


def run_copies(pairs, sems):
    copies = [pltpu.make_async_copy(s, d, sems.at[i]) for i, (s, d) in enumerate(pairs)]
    for copy in copies:
        copy.start()
    for copy in copies:
        copy.wait()


def stage_kernel(z_ref, diag_ref, own_ref, send_ref, corner_ref, sems):
    level, half = level_and_half()
    size = z_ref.shape[0]
    start = pl.multiple_of(level * 2 * size, 2 * size)
    copy = pltpu.make_async_copy(diag_ref.at[:, pl.ds(start, size)], corner_ref, sems.at[0])
    copy.start()
    width = z_ref.shape[1] // 2
    flipped = z_ref[...].T
    low, high = flipped[:width], flipped[width:]
    own_ref[...] = jnp.where(half == 0, low, high)
    send_ref[...] = jnp.where(half == 0, high, low)
    copy.wait()


def inverse_of(tri):
    size = tri.shape[0]
    base = 16
    count = size // base
    rows = lax.broadcasted_iota(jnp.int32, (size, size), 0)
    cols = lax.broadcasted_iota(jnp.int32, (size, size), 1)
    same = (rows // base) == (cols // base)
    folded = jnp.sum(jnp.where(same, tri, 0.0).reshape(count, base, size), axis=0)
    lane = lax.broadcasted_iota(jnp.int32, (base, size), 1) % base
    line = lax.broadcasted_iota(jnp.int32, (base, size), 0)
    spread = jnp.concatenate([jnp.where(lane == k, folded, 0.0) for k in range(base)], axis=0)
    spread = mul(spread, jnp.where(same, 1.0, 0.0))
    rest = jnp.where(lane == line, 1.0, 0.0)
    done = jnp.zeros((base, size), F32)
    for k in range(base):
        column = spread[k * base:(k + 1) * base]
        solved = rest[k:k + 1] / column[k:k + 1]
        done = jnp.where(line == k, solved, done)
        rest = rest - jnp.where(line > k, column, 0.0) * solved
    full = jnp.where(same, jnp.concatenate([done] * count, axis=0), 0.0)
    step = base
    while step < size:
        pair = (rows // (2 * step)) == (cols // (2 * step))
        below = ((rows // step) % 2 == 1) & ((cols // step) % 2 == 0)
        off = jnp.where(pair & below, tri, 0.0)
        full = full - mul(full, mul(off, full))
        step *= 2
    return full


def inverse_kernel(levels, diag_ref, inv_ref, near_ref, far_ref, tile_ref, sems):
    own_row = lax.axis_index("row")
    level, _ = level_and_half()
    size = tile_ref.shape[0]
    width = 2 * size
    strip = size // 2
    core = lax.axis_index("col") % 2
    lines = pl.ds(pl.multiple_of(core * strip, strip), strip)
    pairs = [(diag_ref.at[:, pl.ds(pl.multiple_of(own_row * size, size), size)], tile_ref)]
    for d in range(1, levels):
        block = jnp.maximum(level - d, 0)
        source = diag_ref.at[lines, pl.ds(pl.multiple_of(block * width, width), width)]
        target = near_ref if d == 1 else far_ref.at[:, pl.ds((d - 2) * width, width)]
        pairs.append((source, target))
    copies = [pltpu.make_async_copy(s, t, sems.at[i]) for i, (s, t) in enumerate(pairs)]
    for copy in copies:
        copy.start()
    copies[0].wait()
    inv_ref[...] = inverse_of(tile_ref[...])
    for copy in copies[1:]:
        copy.wait()


def solve_kernel(turn, chunks, depths, *refs):
    (z_own, z_other, inv_own, inv_other, corner_own, corner_other, diag,
     near_a, near_b, far_a, far_b) = refs[:11]
    ups = dict(zip(depths, refs[11:]))
    out, rest, tiles, low, low_other, came, sems = refs[11 + len(depths):]
    level, half = level_and_half()
    core = lax.axis_index("col") % 2
    part, size = rest.shape[1:]
    width = 2 * size
    strip = size // 2
    chunk = turn - level

    @pl.when((chunk >= 0) & (chunk < chunks))
    def _():
        lines = pl.ds(pl.multiple_of(chunk * part, part), part)
        first = [
            (z_own.at[lines], rest.at[0]),
            (z_other.at[lines], rest.at[1]),
            (inv_own, tiles.at[0]),
            (inv_other, tiles.at[1]),
        ]
        first = [pltpu.make_async_copy(s, t, sems.at[i]) for i, (s, t) in enumerate(first)]
        own_corner = pltpu.make_async_copy(corner_own, tiles.at[2], sems.at[4])
        other_corner = pltpu.make_async_copy(corner_other, tiles.at[2], sems.at[4])
        for copy in first:
            copy.start()

        @pl.when(half == 1)
        def _():
            own_corner.start()

        @pl.when(half == 0)
        def _():
            other_corner.start()

        later = {}
        for d in depths:
            block = jnp.maximum(level - d, 0)
            spot = pl.ds((d - 1) * width, width)
            here = pl.ds(pl.multiple_of(core * strip, strip), strip)
            there = pl.ds(pl.multiple_of((1 - core) * strip, strip), strip)
            side_a = near_a if d == 1 else far_a.at[:, pl.ds((d - 2) * width, width)]
            side_b = near_b if d == 1 else far_b.at[:, pl.ds((d - 2) * width, width)]
            pairs = [
                (ups[d], came.at[d - 1]),
                (diag.at[:, pl.ds(pl.multiple_of(block * width, width), width)], low.at[:, spot]),
                (side_a, low_other.at[here, spot]),
                (side_b, low_other.at[there, spot]),
            ]
            later[d] = [
                pltpu.make_async_copy(s, t, sems.at[5 + 4 * (d - 1) + i])
                for i, (s, t) in enumerate(pairs)
            ]

            @pl.when(level >= d)
            def _(d=d):
                for copy in later[d]:
                    copy.start()

        for copy in first:
            copy.wait()
        own_corner.wait()
        for d in reversed(depths):
            @pl.when(level >= d)
            def _(d=d):
                for copy in later[d]:
                    copy.wait()
                spot = pl.ds((d - 1) * width, width)
                rest[0] -= mul_t(came[d - 1], low[:, spot])
                rest[1] -= mul_t(came[d - 1], low_other[:, spot])

        upper = half == 0
        top = mul_t(
            jnp.where(upper, rest[0], rest[1]), jnp.where(upper, tiles[0], tiles[1])
        )
        bottom = jnp.where(upper, rest[1], rest[0]) - mul_t(top, tiles[2])
        out[:, :size] = top
        out[:, size:] = mul_t(bottom, jnp.where(upper, tiles[1], tiles[0]))


def pack_kernel(plan, width, *refs):
    out, sems = refs[-2:]
    level, _ = level_and_half()
    for phase in (0, 1):
        for slot, choices in enumerate(plan):
            target = out.at[:, pl.ds(slot * width, width)]
            for want, index in choices:
                copy = pltpu.make_async_copy(refs[index], target, sems.at[slot])

                @pl.when(level == want)
                def _(copy=copy):
                    copy.start() if phase == 0 else copy.wait()


def finish_kernel(chunks, slots, *refs):
    ins = refs[:4 * chunks]
    norm, high, low, norm_out, lines, sems = refs[4 * chunks:]
    _, half = level_and_half()
    wide = lines.shape[0]
    part = wide // 2 // chunks
    short = ins[0].shape[1]
    copies = []
    for j in range(chunks):
        for side in (0, 1):
            place = jnp.where(half == side, 0, 1) * (wide // 2) + j * part
            spot = pl.ds(pl.multiple_of(place, part), part)
            for piece, columns in ((0, pl.ds(0, short)), (1, pl.ds(short, lines.shape[1] - short))):
                copies.append(pltpu.make_async_copy(
                    ins[4 * j + 2 * side + piece], lines.at[spot, columns], sems.at[len(copies)]))
    for copy in copies:
        copy.start()
    for copy in copies:
        copy.wait()
    total = norm[...]
    depth = high.shape[0] // slots
    for k in range(slots):
        block = lines[:, k * depth:(k + 1) * depth].T
        coarse = block.astype(BF16)
        high[k * depth:(k + 1) * depth] = coarse
        low[k * depth:(k + 1) * depth] = (block - coarse.astype(F32)).astype(BF16)
        total = total + jnp.sum(block * block, axis=0, keepdims=True)
    norm_out[...] = total


def trail_kernel(flips, *refs):
    parts = refs[:len(flips)]
    z_ref, high, low = refs[len(flips):len(flips) + 3]
    out = refs[-1]
    own_col = lax.axis_index("col")
    total = z_ref[...]
    for flip, part in zip(flips, parts):
        depth = part.shape[1]
        lines = pl.ds(pl.multiple_of(lax.bitwise_xor(own_col, flip) * depth, depth), depth)
        value = part[...]
        coarse = value.astype(BF16)
        fine = (value - coarse.astype(F32)).astype(BF16)
        high_lines = high[lines, :]
        total = total - jnp.dot(coarse, high_lines, preferred_element_type=F32)
        total = total - jnp.dot(coarse, low[lines, :], preferred_element_type=F32)
        total = total - jnp.dot(fine, high_lines, preferred_element_type=F32)
    out[...] = total


def tie_kernel(x_ref, token_ref, out_ref):
    del x_ref, token_ref, out_ref


def tie(x, token):
    return pl.pallas_call(
        tie_kernel,
        out_shape=jax.ShapeDtypeStruct(x.shape, x.dtype),
        in_specs=[ANY, ANY],
        out_specs=ANY,
        input_output_aliases={0: 0},
    )(x, token)


def struct(*shape, dtype=F32):
    return jax.ShapeDtypeStruct(shape, dtype)


def forward_substitution(diag_block, z_panel, norm_sq):
    rows = lax.axis_size("row")
    levels = rows // 2
    cols = lax.axis_size("col")
    size, full = diag_block.shape
    wide = z_panel.shape[1]
    width, half_wide, strip = 2 * size, wide // 2, size // 2
    part = half_wide // CHUNKS
    dma = pltpu.SemaphoreType.DMA

    swap = [(i, i ^ 1) for i in range(rows)]
    cores = [(i, i ^ 1) for i in range(cols)]

    z_own, z_send, corner = pl.pallas_call(
        stage_kernel,
        out_shape=(struct(half_wide, size), struct(half_wide, size), struct(size, size)),
        in_specs=[VMEM, ANY],
        out_specs=(VMEM, VMEM, ANY),
        scratch_shapes=[dma((1,))],
        compiler_params=params(),
    )(z_panel, diag_block)
    z_other = lax.ppermute(z_send, "row", swap)
    corner_other = lax.ppermute(corner, "row", [p for p in swap if p[0] % 2 == 1])
    inv, near, far = pl.pallas_call(
        lambda *refs: inverse_kernel(levels, *refs),
        out_shape=(struct(size, size), struct(strip, width), struct(strip, width * (levels - 2))),
        in_specs=[ANY],
        out_specs=(VMEM, ANY, ANY),
        scratch_shapes=[pltpu.VMEM((size, size), F32), dma((levels,))],
        compiler_params=params(),
    )(diag_block)
    inv_other = lax.ppermute(inv, "row", swap)
    near_a = lax.ppermute(near, "row", [p for p in swap if p[0] >= 2])
    near_b = lax.ppermute(near_a, "col", cores)
    far_a = lax.ppermute(far, "row", [p for p in swap if p[0] >= 4])
    far_b = lax.ppermute(far_a, "col", cores)

    solved, ups, downs = {}, {}, {}
    for turn in range(levels - 1 + CHUNKS):
        depths = [d for d in range(1, levels) if (d, turn - d) in ups]
        args = [z_own, z_other, inv, inv_other, corner, corner_other, diag_block,
                near_a, near_b, far_a, far_b] + [ups[d, turn - d] for d in depths]
        deep = max(depths, default=1)
        solved[turn] = pl.pallas_call(
            lambda *refs, turn=turn, depths=depths: solve_kernel(turn, CHUNKS, depths, *refs),
            out_shape=struct(part, width),
            in_specs=[ANY] * len(args),
            out_specs=VMEM,
            scratch_shapes=[
                pltpu.VMEM((2, part, size), F32),
                pltpu.VMEM((3, size, size), F32),
                pltpu.VMEM((size, deep * width), F32),
                pltpu.VMEM((size, deep * width), F32),
                pltpu.VMEM((deep, part, width), F32),
                dma((5 + 4 * deep,)),
            ],
            compiler_params=params(),
        )(*args)
        busy = [z for z in range(levels) if 0 <= turn - z < CHUNKS]
        for d in range(1, levels):
            up = [(2 * z + y, 2 * (z + d) + y) for z in busy for y in (0, 1) if z + d < levels]
            down = [(2 * z + y, 2 * (z - d) + y) for z in busy for y in (0, 1) if z - d >= 0]
            if up:
                ups[d, turn] = lax.ppermute(solved[turn], "row", up)
            if down:
                downs[d, turn] = lax.ppermute(solved[turn], "row", down)

    def pack(chunk, wanted):
        args, plan = [], []
        for level in wanted:
            turn = level + chunk
            choices = [(level, len(args))]
            args.append(solved[turn])
            for z in range(levels):
                if z != level:
                    choices.append((z, len(args)))
                    args.append(ups[z - level, turn] if z > level else downs[level - z, turn])
            plan.append(choices)
        return pl.pallas_call(
            lambda *refs: pack_kernel(plan, width, *refs),
            out_shape=struct(part, width * len(wanted)),
            in_specs=[ANY] * len(args),
            out_specs=ANY,
            scratch_shapes=[dma((len(wanted),))],
            compiler_params=params(),
        )(*args)

    ready = []
    for chunk in range(CHUNKS):
        early = pack(chunk, range(levels - 1))
        last = pack(chunk, [levels - 1])
        ready += [early, last, lax.ppermute(early, "row", swap), lax.ppermute(last, "row", swap)]

    high, low, norm_out = pl.pallas_call(
        lambda *refs: finish_kernel(CHUNKS, levels, *refs),
        out_shape=(struct(full, wide, dtype=BF16), struct(full, wide, dtype=BF16), struct(1, wide)),
        in_specs=[ANY] * len(ready) + [VMEM],
        out_specs=(VMEM, VMEM, VMEM),
        scratch_shapes=[pltpu.VMEM((wide, full), F32), dma((len(ready),))],
        compiler_params=params(),
    )(*ready, norm_sq.reshape(1, wide))
    return high, low, norm_out.reshape(wide), solved[levels - 2 + CHUNKS]


def trailing(out, piece_start, piece_rows, panels, pieces, z_trail, high, low):
    rows, wide = z_trail.shape
    depth = high.shape[0]
    tile = min(256, piece_rows)
    skip = piece_start // tile
    flips = [flip for flip, _ in panels] + [flip for flip, _ in pieces]
    args = [x for _, x in panels] + [x for _, x in pieces]
    in_specs = [pl.BlockSpec((tile, x.shape[1]), lambda i: (i + skip, 0)) for _, x in panels]
    in_specs += [pl.BlockSpec((tile, x.shape[1]), lambda i: (i, 0)) for _, x in pieces]
    in_specs += [pl.BlockSpec((tile, wide), lambda i: (i + skip, 0))]
    in_specs += [pl.BlockSpec((depth, wide), lambda i: (0, 0))] * 2
    args += [z_trail, high, low]
    aliases = {}
    if out is not None:
        aliases = {len(args): 0}
        args.append(out)
        in_specs.append(ANY)
    return pl.pallas_call(
        lambda *refs: trail_kernel(flips, *refs),
        grid=(piece_rows // tile,),
        out_shape=struct(rows, wide),
        in_specs=in_specs,
        out_specs=pl.BlockSpec((tile, wide), lambda i: (i + skip, 0)),
        input_output_aliases=aliases,
        compiler_params=params(),
        cost_estimate=pl.CostEstimate(
            flops=6 * piece_rows * depth * wide,
            bytes_accessed=4 * piece_rows * (depth + 2 * wide),
            transcendentals=0,
        ),
    )(*args)


def shards(diag_block, z_panel, panel_below, z_trail, norm_sq):
    cols = lax.axis_size("col")
    height = panel_below.shape[0]
    unit = height // sum(ROW_PIECES)
    bounds = []
    start = 0
    for count in ROW_PIECES:
        bounds.append((start, count * unit))
        start += count * unit

    def flipped(x, flip):
        return lax.ppermute(x, "col", [(i, i ^ flip) for i in range(cols)])

    crossed = [
        [(flip, flipped(panel_below[s:s + n], flip)) for flip in range(2, cols, 2)]
        for s, n in bounds
    ]
    mate = flipped(panel_below, 1)
    high, low, norm_out, token = forward_substitution(diag_block, z_panel, norm_sq)
    panels = [(0, panel_below), (1, mate)]
    out = None
    pieces = []
    for index, piece in enumerate(crossed):
        hold = high if index == len(crossed) - 1 else token
        piece = [(flip, tie(x, hold)) for flip, x in piece]
        pieces.append(piece + [(flip ^ 1, flipped(x, 1)) for flip, x in piece])
    for (s, n), piece in zip(bounds, pieces):
        out = trailing(out, s, n, panels, piece, z_trail, high, low)
    return (norm_out, out)


def solution(mesh):
    return jax.shard_map(
        shards,
        mesh=mesh,
        in_specs=(P("row", None), P("row", "col"), P("row", "col"), P("row", "col"), P("col")),
        out_specs=(P("col"), P("row", "col")),
        check_vma=False,
    )
```

```python
import jax
import jax.numpy as jnp
from jax import lax
from jax.experimental import pallas as pl
from jax.experimental.pallas import tpu as pltpu
from jax.sharding import PartitionSpec as P

F32 = jnp.float32
BF16 = jnp.bfloat16
HIGHEST = lax.Precision.HIGHEST
ANY = pl.BlockSpec(memory_space=pl.ANY)
VMEM = pl.BlockSpec(memory_space=pltpu.VMEM)
LIMIT = 62 * 1024 * 1024
RETURNS = 2
TINY = pl.CostEstimate(flops=1, bytes_accessed=1, transcendentals=0)


def params():
    return pltpu.CompilerParams(vmem_limit_bytes=LIMIT)


def mul(a, b):
    return jnp.dot(a, b, precision=HIGHEST, preferred_element_type=F32)


def mul_t(a, b):
    return lax.dot_general(
        a, b, (((1,), (1,)), ((), ())), precision=HIGHEST, preferred_element_type=F32
    )


def level_and_half():
    own_row = lax.axis_index("row")
    return own_row // 2, own_row % 2


def run_copies(pairs, sems):
    copies = [pltpu.make_async_copy(s, d, sems.at[i]) for i, (s, d) in enumerate(pairs)]
    for copy in copies:
        copy.start()
    for copy in copies:
        copy.wait()


def stage_kernel(z_ref, diag_ref, own_ref, send_ref, corner_ref, panel, sems):
    level, half = level_and_half()
    size = z_ref.shape[0]
    start = pl.multiple_of(level * 2 * size, 2 * size)
    run_copies([(z_ref, panel), (diag_ref.at[:, pl.ds(start, size)], corner_ref)], sems)
    width = z_ref.shape[1] // 2
    flipped = panel[...].T
    low, high = flipped[:width], flipped[width:]
    own_ref[...] = jnp.where(half == 0, low, high)
    send_ref[...] = jnp.where(half == 0, high, low)


def inverse_of(tri):
    size = tri.shape[0]
    base = 16
    count = size // base
    rows = lax.broadcasted_iota(jnp.int32, (size, size), 0)
    cols = lax.broadcasted_iota(jnp.int32, (size, size), 1)
    same = (rows // base) == (cols // base)
    folded = jnp.sum(jnp.where(same, tri, 0.0).reshape(count, base, size), axis=0)
    lane = lax.broadcasted_iota(jnp.int32, (base, size), 1) % base
    line = lax.broadcasted_iota(jnp.int32, (base, size), 0)
    spread = jnp.concatenate([jnp.where(lane == k, folded, 0.0) for k in range(base)], axis=0)
    spread = mul(spread, jnp.where(same, 1.0, 0.0))
    rest = jnp.where(lane == line, 1.0, 0.0)
    done = jnp.zeros((base, size), F32)
    for k in range(base):
        column = spread[k * base:(k + 1) * base]
        solved = rest[k:k + 1] / column[k:k + 1]
        done = jnp.where(line == k, solved, done)
        rest = rest - jnp.where(line > k, column, 0.0) * solved
    full = jnp.where(same, jnp.concatenate([done] * count, axis=0), 0.0)
    step = base
    while step < size:
        pair = (rows // (2 * step)) == (cols // (2 * step))
        below = ((rows // step) % 2 == 1) & ((cols // step) % 2 == 0)
        off = jnp.where(pair & below, tri, 0.0)
        full = full - mul(full, mul(off, full))
        step *= 2
    return full


def inverse_kernel(diag_ref, token_ref, inv_ref, tile_ref, sems):
    del token_ref
    own_row = lax.axis_index("row")
    size = tile_ref.shape[0]
    source = diag_ref.at[:, pl.ds(pl.multiple_of(own_row * size, size), size)]
    run_copies([(source, tile_ref)], sems)
    inv_ref[...] = inverse_of(tile_ref[...])


def strips_kernel(distances, diag_ref, *refs):
    out_ref, sems = refs[-2:]
    level, _ = level_and_half()
    strip = out_ref.shape[0]
    width = 4 * strip
    core = lax.axis_index("col") % 2
    lines = pl.ds(pl.multiple_of(core * strip, strip), strip)
    pairs = []
    for slot, d in enumerate(distances):
        block = jnp.maximum(level - d, 0)
        source = diag_ref.at[lines, pl.ds(pl.multiple_of(block * width, width), width)]
        pairs.append((source, out_ref.at[:, pl.ds(slot * width, width)]))
    run_copies(pairs, sems)


def mul_t3(a, b):
    def parts(x):
        coarse = x.astype(BF16)
        return coarse, (x - coarse.astype(F32)).astype(BF16)

    def dot(x, y):
        return lax.dot_general(x, y, (((1,), (1,)), ((), ())), preferred_element_type=F32)

    (a_high, a_low), (b_high, b_low) = parts(a), parts(b)
    return dot(a_high, b_high) + dot(a_high, b_low) + dot(a_low, b_high)


def solve_kernel(turn, n_refs, *refs):
    z_own, z_other, inv_own, inv_other, corner_own, corner_other, diag, *rest_refs = refs[:n_refs]
    came = rest_refs[:turn]
    strips = rest_refs[turn:turn + 2 * min(turn, 2)]
    outs = refs[n_refs:-6]
    rest, tiles, low, low_other, earlier, sems = refs[-6:]
    level, half = level_and_half()
    core = lax.axis_index("col") % 2
    lines, size = rest.shape[1:]
    width = 2 * size
    strip = size // 2

    @pl.when(level == turn)
    def _():
        pairs = [
            (z_own, rest.at[0]),
            (z_other, rest.at[1]),
            (inv_own, tiles.at[0]),
            (inv_other, tiles.at[1]),
        ]
        here = pl.ds(pl.multiple_of(core * strip, strip), strip)
        there = pl.ds(pl.multiple_of((1 - core) * strip, strip), strip)
        if turn:
            pairs.append((diag.at[:, pl.ds(0, turn * width)], low))
        for d in range(1, turn + 1):
            spot = pl.ds((turn - d) * width, width)
            pairs.append((came[d - 1], earlier.at[:, spot]))
            for side, place in zip(strips[:2] if d == 1 else strips[2:], (here, there)):
                if d > 1:
                    side = side.at[:, pl.ds((d - 2) * width, width)]
                pairs.append((side, low_other.at[place, spot]))
        copies = [pltpu.make_async_copy(s, t, sems.at[i + 1]) for i, (s, t) in enumerate(pairs)]
        own_corner = pltpu.make_async_copy(corner_own, tiles.at[2], sems.at[0])
        other_corner = pltpu.make_async_copy(corner_other, tiles.at[2], sems.at[0])
        for copy in copies:
            copy.start()

        @pl.when(half == 1)
        def _():
            own_corner.start()

        @pl.when(half == 0)
        def _():
            other_corner.start()

        for copy in copies:
            copy.wait()
        own_corner.wait()
        first, second = rest[0], rest[1]
        if turn:
            first = first - mul_t3(earlier[...], low[...])
            second = second - mul_t3(earlier[...], low_other[...])
        upper = half == 0
        top = mul_t(jnp.where(upper, first, second), jnp.where(upper, tiles[0], tiles[1]))
        bottom = jnp.where(upper, second, first) - mul_t(top, tiles[2])
        bottom = mul_t(bottom, jnp.where(upper, tiles[1], tiles[0]))
        part = outs[0].shape[0]
        for q, out in enumerate(outs):
            out[:, :size] = top[q * part:(q + 1) * part]
            out[:, size:] = bottom[q * part:(q + 1) * part]


def pick_kernel(levels, *refs):
    out, sems = refs[-2:]
    level, _ = level_and_half()
    for z in range(levels):
        @pl.when(level == z)
        def _(z=z):
            run_copies([(refs[z], out)], sems)


def product(value, high, low):
    coarse = value.astype(BF16)
    fine = (value - coarse.astype(F32)).astype(BF16)
    total = jnp.dot(coarse, high, preferred_element_type=F32)
    total += jnp.dot(coarse, low, preferred_element_type=F32)
    return total + jnp.dot(fine, high, preferred_element_type=F32)


def update_kernel(plan, flips, tile, n_refs, *refs):
    ins = refs[:2 * len(plan)]
    norm, partial = refs[2 * len(plan):2 * len(plan) + 2]
    parts = refs[2 * len(plan) + 2:2 * len(plan) + 2 + len(flips)]
    norm_out, out, lines, high, low, panel, sems, panel_sems = refs[n_refs:]
    own_col = lax.axis_index("col")
    _, half = level_and_half()
    step = pl.program_id(0)
    rows, depth = parts[0].shape
    tiles = rows // tile
    wide, span = lines.shape
    width = span // len({level for level, _, _ in plan})
    count = span // depth
    first = min(level for level, _, _ in plan) * (width // depth)

    def panel_copies(act):
        for flip, part in zip(flips, parts):
            slot = lax.bitwise_xor(own_col, flip) - first

            @pl.when((slot >= 0) & (slot < count))
            def _(part=part, slot=slot):
                for i in range(tiles):
                    spot = pl.ds(i * tile, tile)
                    act(i, pltpu.make_async_copy(
                        part.at[spot], panel.at[slot, spot], panel_sems.at[i, slot]))

    @pl.when(step == 0)
    def _():
        pairs = []
        for index, (_, place, line) in enumerate(plan):
            for side in (0, 1):
                ref = ins[2 * index + side]
                number = ref.shape[0]
                start = jnp.where(half == side, 0, wide // 2) + line
                pairs.append((ref, lines.at[
                    pl.ds(pl.multiple_of(start, number), number), pl.ds(place * width, width)]))
        copies = [pltpu.make_async_copy(s, t, sems.at[i]) for i, (s, t) in enumerate(pairs)]
        for copy in copies:
            copy.start()
        panel_copies(lambda i, copy: copy.start())
        for copy in copies:
            copy.wait()
        total = norm[...]
        for k in range(span // width):
            block = lines[:, k * width:(k + 1) * width].T
            coarse = block.astype(BF16)
            high[k * width:(k + 1) * width] = coarse
            low[k * width:(k + 1) * width] = (block - coarse.astype(F32)).astype(BF16)
            total = total + jnp.sum(block * block, axis=0, keepdims=True)
        norm_out[...] = total

    def wait(i, copy):
        @pl.when(step == i)
        def _():
            copy.wait()

    panel_copies(wait)
    here = pl.ds(pl.multiple_of(step * tile, tile), tile)
    total = partial[...]
    for k in range(count):
        spot = slice(k * depth, (k + 1) * depth)
        total = total - product(panel[k, here, :], high[spot], low[spot])
    out[...] = total


def tie_kernel(x_ref, token_ref, out_ref):
    del x_ref, token_ref, out_ref


def tie(x, token):
    return pl.pallas_call(
        tie_kernel,
        out_shape=jax.ShapeDtypeStruct(x.shape, x.dtype),
        in_specs=[ANY, ANY],
        out_specs=ANY,
        input_output_aliases={0: 0},
        cost_estimate=TINY,
    )(x, token)


def struct(*shape, dtype=F32):
    return jax.ShapeDtypeStruct(shape, dtype)


def forward_substitution(diag_block, z_panel):
    rows = lax.axis_size("row")
    levels = rows // 2
    last = levels - 1
    cols = lax.axis_size("col")
    size, full = diag_block.shape
    wide = z_panel.shape[1]
    width, half_wide, strip = 2 * size, wide // 2, size // 2
    dma = pltpu.SemaphoreType.DMA

    swap = [(i, i ^ 1) for i in range(rows)]
    cores = [(i, i ^ 1) for i in range(cols)]

    def move(x, source, target):
        return lax.ppermute(x, "row", [(2 * source + y, 2 * target + y) for y in (0, 1)])

    def strips(distances, *tokens):
        return pl.pallas_call(
            lambda *refs: strips_kernel(distances, *refs),
            out_shape=struct(strip, width * len(distances)),
            in_specs=[ANY] * (1 + len(tokens)),
            out_specs=VMEM,
            scratch_shapes=[dma((len(distances),))],
            compiler_params=params(),
            cost_estimate=TINY,
        )(diag_block, *tokens)

    z_own, z_send, corner = pl.pallas_call(
        stage_kernel,
        out_shape=(struct(half_wide, size), struct(half_wide, size), struct(size, size)),
        in_specs=[ANY, ANY],
        out_specs=(VMEM, VMEM, VMEM),
        scratch_shapes=[pltpu.VMEM((size, wide), F32), dma((2,))],
        compiler_params=params(),
        cost_estimate=TINY,
    )(z_panel, diag_block)
    z_other = lax.ppermute(z_send, "row", swap)
    corner_other = lax.ppermute(corner, "row", [p for p in swap if p[0] % 2 == 1])
    inv = pl.pallas_call(
        inverse_kernel,
        out_shape=struct(size, size),
        in_specs=[ANY, ANY],
        out_specs=VMEM,
        scratch_shapes=[pltpu.VMEM((size, size), F32), dma((1,))],
        compiler_params=params(),
        cost_estimate=TINY,
    )(diag_block, z_send)
    inv_other = lax.ppermute(inv, "row", swap)
    near_a = lax.ppermute(
        strips([1], inv_other, z_other, corner_other), "row", [p for p in swap if p[0] >= 2])

    def solve(turn, came, strip_pairs, token, n_out=1):
        args = [z_own, z_other, inv, inv_other, corner, corner_other, diag_block]
        args += [*came, *strip_pairs]
        args += [token] if token is not None else []
        deep = max(turn, 1) * width
        return pl.pallas_call(
            lambda *refs: solve_kernel(turn, len(args), *refs),
            out_shape=[struct(half_wide // n_out, width)] * n_out,
            in_specs=[ANY] * len(args),
            out_specs=[VMEM] * n_out,
            scratch_shapes=[
                pltpu.VMEM((2, half_wide, size), F32),
                pltpu.VMEM((3, size, size), F32),
                pltpu.VMEM((size, deep), F32),
                pltpu.VMEM((size, deep), F32),
                pltpu.VMEM((half_wide, deep), F32),
                dma((6 + 3 * turn,)),
            ],
            compiler_params=params(),
            cost_estimate=TINY,
        )(*args)

    def pick(sources, *tokens):
        args = [sources[z] for z in range(levels)]
        return pl.pallas_call(
            lambda *refs: pick_kernel(levels, *refs),
            out_shape=struct(*args[0].shape),
            in_specs=[ANY] * (levels + len(tokens)),
            out_specs=VMEM,
            scratch_shapes=[dma((1,))],
            compiler_params=params(),
            cost_estimate=TINY,
        )(*args, *tokens)

    held, pieces = {}, {}
    strip_pairs = ()
    token = None

    def share(level, index, tokens):
        mine = pick(pieces[level][index], *tokens)
        return mine, lax.ppermute(mine, "row", swap)

    for turn in range(levels):
        came = [held[turn - d][turn] for d in range(1, turn + 1)]
        for k in range(turn):
            if turn < last:
                held[k][turn + 1] = move(held[k][turn], turn, turn + 1)
        own = solve(turn, came, strip_pairs, token, RETURNS if turn == last else 1)
        token = own[0]
        if turn < last:
            held[turn] = {turn: own[0], turn + 1: move(own[0], turn, turn + 1)}
        pieces[turn] = []
        for part in own:
            place = {turn: part}
            for z in range(turn - 1, -1, -1):
                place[z] = move(place[z + 1], z + 1, z) if turn == last else move(part, turn, z)
            pieces[turn].append(place)
        if turn == 0:
            strip_pairs = (near_a, lax.ppermute(tie(near_a, token), "col", cores))
        if turn == 1:
            far_a = lax.ppermute(
                strips(list(range(2, levels)), token), "row", [p for p in swap if p[0] >= 4])
            strip_pairs += (far_a, lax.ppermute(far_a, "col", cores))
        if turn == last - 1:
            for k in range(last - 1):
                pieces[k][0].update(held[k])
                shared = share(k, 0, [token])
                pieces[k] = [shared]
                token = shared[0]
    pieces[last - 1][0].update(held[last - 1])
    shared = share(last - 1, 0, [token])
    pieces[last - 1] = [shared]
    token = shared[0]
    return pieces, share, token


def shards(diag_block, z_panel, panel_below, z_trail, norm_sq):
    cols = lax.axis_size("col")
    levels = lax.axis_size("row") // 2
    last = levels - 1
    rows, wide = z_trail.shape
    width = 2 * diag_block.shape[0]
    tile = min(512, rows)
    depth = panel_below.shape[1]
    dma = pltpu.SemaphoreType.DMA

    def flipped(x, flip):
        return lax.ppermute(x, "col", [(i, i ^ flip) for i in range(cols)])

    crossed = {flip: flipped(panel_below, flip) for flip in range(2, cols, 2)}
    panels = {0: panel_below, 1: flipped(panel_below, 1)}
    pieces, share, token = forward_substitution(diag_block, z_panel)
    for flip, x in crossed.items():
        panels[flip] = tie(x, token)
        panels[flip ^ 1] = flipped(panels[flip], 1)
    flips = list(panels)
    slabs = [panels[flip] for flip in flips]

    def update(wanted, norm, out):
        plan, args = [], []
        for place, level in enumerate(wanted):
            line = 0
            for pair in pieces[level]:
                plan.append((level, place, line))
                args += pair
                line += pair[0].shape[0]
        first = out is z_trail
        span = width * len(wanted)
        aliases = {} if first else {len(args) + 1: 1}
        args += [norm, out, *slabs]
        line = pl.BlockSpec((1, wide), lambda i: (0, 0))
        whole = pl.BlockSpec((tile, wide), lambda i: (i, 0))
        return pl.pallas_call(
            lambda *refs: update_kernel(plan, flips, tile, len(args), *refs),
            grid=(rows // tile,),
            out_shape=(struct(1, wide), struct(rows, wide)),
            in_specs=[ANY] * (2 * len(plan)) + [line, whole] + [ANY] * len(slabs),
            out_specs=(line, whole),
            scratch_shapes=[
                pltpu.VMEM((wide, span), F32),
                pltpu.VMEM((span, wide), BF16),
                pltpu.VMEM((span, wide), BF16),
                pltpu.VMEM((span // depth, rows, depth), F32),
                dma((2 * len(plan),)),
                dma((rows // tile, span // depth)),
            ],
            input_output_aliases=aliases,
            compiler_params=params(),
            cost_estimate=TINY,
        )(*args)

    norm, out = update(range(last - 1), norm_sq.reshape(1, wide), z_trail)
    pairs = []
    for index in range(RETURNS):
        pairs.append(share(last, index, [token, norm]))
        token = pairs[-1][0]
    pieces[last] = pairs
    norm, out = update([last - 1], norm, out)
    norm, out = update([last], norm, out)
    return (norm.reshape(wide), out)


def solution(mesh):
    return jax.shard_map(
        shards,
        mesh=mesh,
        in_specs=(P("row", None), P("row", "col"), P("row", "col"), P("row", "col"), P("col")),
        out_specs=(P("col"), P("row", "col")),
        check_vma=False,
    )
```

```python
import jax
import jax.numpy as jnp
from jax import lax
from jax.experimental import pallas as pl
from jax.experimental.pallas import tpu as pltpu
from jax.sharding import PartitionSpec as P

F32 = jnp.float32
BF16 = jnp.bfloat16
HIGHEST = lax.Precision.HIGHEST
ANY = pl.BlockSpec(memory_space=pl.ANY)
VMEM = pl.BlockSpec(memory_space=pltpu.VMEM)
LIMIT = 62 * 1024 * 1024
RETURNS = 2
TINY = pl.CostEstimate(flops=1, bytes_accessed=1, transcendentals=0)


def params(limit=LIMIT):
    return pltpu.CompilerParams(vmem_limit_bytes=limit)


def mul(a, b):
    return jnp.dot(a, b, precision=HIGHEST, preferred_element_type=F32)


def mul_t(a, b):
    return lax.dot_general(
        a, b, (((1,), (1,)), ((), ())), precision=HIGHEST, preferred_element_type=F32
    )


def level_and_half():
    own_row = lax.axis_index("row")
    return own_row // 2, own_row % 2


def run_copies(pairs, sems):
    copies = [pltpu.make_async_copy(s, d, sems.at[i]) for i, (s, d) in enumerate(pairs)]
    for copy in copies:
        copy.start()
    for copy in copies:
        copy.wait()


def stage_kernel(z_ref, diag_ref, own_ref, send_ref, corner_ref, panel, sems):
    level, half = level_and_half()
    size = z_ref.shape[0]
    start = pl.multiple_of(level * 2 * size, 2 * size)
    run_copies([(z_ref, panel), (diag_ref.at[:, pl.ds(start, size)], corner_ref)], sems)
    width = z_ref.shape[1] // 2
    flipped = panel[...].T
    low, high = flipped[:width], flipped[width:]
    own_ref[...] = jnp.where(half == 0, low, high)
    send_ref[...] = jnp.where(half == 0, high, low)


def inverse_of(tri):
    size = tri.shape[0]
    base = 16
    count = size // base
    rows = lax.broadcasted_iota(jnp.int32, (size, size), 0)
    cols = lax.broadcasted_iota(jnp.int32, (size, size), 1)
    same = (rows // base) == (cols // base)
    folded = jnp.sum(jnp.where(same, tri, 0.0).reshape(count, base, size), axis=0)
    lane = lax.broadcasted_iota(jnp.int32, (base, size), 1) % base
    line = lax.broadcasted_iota(jnp.int32, (base, size), 0)
    spread = jnp.concatenate([jnp.where(lane == k, folded, 0.0) for k in range(base)], axis=0)
    spread = mul(spread, jnp.where(same, 1.0, 0.0))
    rest = jnp.where(lane == line, 1.0, 0.0)
    done = jnp.zeros((base, size), F32)
    for k in range(base):
        column = spread[k * base:(k + 1) * base]
        solved = rest[k:k + 1] / column[k:k + 1]
        done = jnp.where(line == k, solved, done)
        rest = rest - jnp.where(line > k, column, 0.0) * solved
    full = jnp.where(same, jnp.concatenate([done] * count, axis=0), 0.0)
    step = base
    while step < size:
        pair = (rows // (2 * step)) == (cols // (2 * step))
        below = ((rows // step) % 2 == 1) & ((cols // step) % 2 == 0)
        off = jnp.where(pair & below, tri, 0.0)
        full = full - mul(full, mul(off, full))
        step *= 2
    return full


def inverse_kernel(diag_ref, token_ref, inv_ref, tile_ref, sems):
    del token_ref
    own_row = lax.axis_index("row")
    size = tile_ref.shape[0]
    source = diag_ref.at[:, pl.ds(pl.multiple_of(own_row * size, size), size)]
    run_copies([(source, tile_ref)], sems)
    inv_ref[...] = inverse_of(tile_ref[...])


def strips_kernel(distances, diag_ref, *refs):
    out_ref, sems = refs[-2:]
    level, _ = level_and_half()
    strip = out_ref.shape[0]
    width = 4 * strip
    core = lax.axis_index("col") % 2
    lines = pl.ds(pl.multiple_of(core * strip, strip), strip)
    pairs = []
    for slot, d in enumerate(distances):
        block = jnp.maximum(level - d, 0)
        source = diag_ref.at[lines, pl.ds(pl.multiple_of(block * width, width), width)]
        pairs.append((source, out_ref.at[:, pl.ds(slot * width, width)]))
    run_copies(pairs, sems)


def mul_t3(a, b):
    def parts(x):
        coarse = x.astype(BF16)
        return coarse, (x - coarse.astype(F32)).astype(BF16)

    def dot(x, y):
        return lax.dot_general(x, y, (((1,), (1,)), ((), ())), preferred_element_type=F32)

    (a_high, a_low), (b_high, b_low) = parts(a), parts(b)
    return dot(a_high, b_high) + dot(a_high, b_low) + dot(a_low, b_high)


def solve_kernel(turn, n_refs, *refs):
    z_own, z_other, inv_own, inv_other, corner_own, corner_other, diag, *rest_refs = refs[:n_refs]
    came = rest_refs[:turn]
    strips = rest_refs[turn:turn + 2 * min(turn, 2)]
    outs = refs[n_refs:-6]
    rest, tiles, low, low_other, earlier, sems = refs[-6:]
    level, half = level_and_half()
    core = lax.axis_index("col") % 2
    lines, size = rest.shape[1:]
    width = 2 * size
    strip = size // 2

    @pl.when(level == turn)
    def _():
        pairs = [
            (z_own, rest.at[0]),
            (z_other, rest.at[1]),
            (inv_own, tiles.at[0]),
            (inv_other, tiles.at[1]),
        ]
        here = pl.ds(pl.multiple_of(core * strip, strip), strip)
        there = pl.ds(pl.multiple_of((1 - core) * strip, strip), strip)
        if turn:
            pairs.append((diag.at[:, pl.ds(0, turn * width)], low))
        for d in range(1, turn + 1):
            spot = pl.ds((turn - d) * width, width)
            pairs.append((came[d - 1], earlier.at[:, spot]))
            for side, place in zip(strips[:2] if d == 1 else strips[2:], (here, there)):
                if d > 1:
                    side = side.at[:, pl.ds((d - 2) * width, width)]
                pairs.append((side, low_other.at[place, spot]))
        copies = [pltpu.make_async_copy(s, t, sems.at[i + 1]) for i, (s, t) in enumerate(pairs)]
        own_corner = pltpu.make_async_copy(corner_own, tiles.at[2], sems.at[0])
        other_corner = pltpu.make_async_copy(corner_other, tiles.at[2], sems.at[0])
        for copy in copies:
            copy.start()

        @pl.when(half == 1)
        def _():
            own_corner.start()

        @pl.when(half == 0)
        def _():
            other_corner.start()

        for copy in copies:
            copy.wait()
        own_corner.wait()
        first, second = rest[0], rest[1]
        if turn:
            first = first - mul_t3(earlier[...], low[...])
            second = second - mul_t3(earlier[...], low_other[...])
        upper = half == 0
        top = mul_t(jnp.where(upper, first, second), jnp.where(upper, tiles[0], tiles[1]))
        bottom = jnp.where(upper, second, first) - mul_t(top, tiles[2])
        bottom = mul_t(bottom, jnp.where(upper, tiles[1], tiles[0]))
        part = outs[0].shape[0]
        for q, out in enumerate(outs):
            out[:, :size] = top[q * part:(q + 1) * part]
            out[:, size:] = bottom[q * part:(q + 1) * part]


def pick_kernel(levels, *refs):
    out, sems = refs[-2:]
    level, _ = level_and_half()
    for z in range(levels):
        @pl.when(level == z)
        def _(z=z):
            run_copies([(refs[z], out)], sems)


def product(value, high, low):
    coarse = value.astype(BF16)
    fine = (value - coarse.astype(F32)).astype(BF16)
    total = jnp.dot(coarse, high, preferred_element_type=F32)
    total += jnp.dot(coarse, low, preferred_element_type=F32)
    return total + jnp.dot(fine, high, preferred_element_type=F32)


def update_kernel(plan, flips, tile, n_refs, *refs):
    ins = refs[:2 * len(plan)]
    norm, partial = refs[2 * len(plan):2 * len(plan) + 2]
    parts = refs[2 * len(plan) + 2:2 * len(plan) + 2 + len(flips)]
    norm_out, out, lines, high, low, panel, sems, panel_sems = refs[n_refs:]
    own_col = lax.axis_index("col")
    _, half = level_and_half()
    step = pl.program_id(0)
    rows, depth = parts[0].shape
    tiles = rows // tile
    wide, span = lines.shape
    width = span // len({level for level, _, _ in plan})
    count = span // depth
    first = min(level for level, _, _ in plan) * (width // depth)

    def panel_copies(act):
        for flip, part in zip(flips, parts):
            slot = lax.bitwise_xor(own_col, flip) - first

            @pl.when((slot >= 0) & (slot < count))
            def _(part=part, slot=slot):
                for i in range(tiles):
                    spot = pl.ds(i * tile, tile)
                    act(i, pltpu.make_async_copy(
                        part.at[spot], panel.at[slot, spot], panel_sems.at[i, slot]))

    @pl.when(step == 0)
    def _():
        pairs = []
        for index, (_, place, line) in enumerate(plan):
            for side in (0, 1):
                ref = ins[2 * index + side]
                number = ref.shape[0]
                start = jnp.where(half == side, 0, wide // 2) + line
                pairs.append((ref, lines.at[
                    pl.ds(pl.multiple_of(start, number), number), pl.ds(place * width, width)]))
        copies = [pltpu.make_async_copy(s, t, sems.at[i]) for i, (s, t) in enumerate(pairs)]
        for copy in copies:
            copy.start()
        panel_copies(lambda i, copy: copy.start())
        for copy in copies:
            copy.wait()
        total = norm[...]
        for k in range(span // width):
            block = lines[:, k * width:(k + 1) * width].T
            coarse = block.astype(BF16)
            high[k * width:(k + 1) * width] = coarse
            low[k * width:(k + 1) * width] = (block - coarse.astype(F32)).astype(BF16)
            total = total + jnp.sum(block * block, axis=0, keepdims=True)
        norm_out[...] = total

    def wait(i, copy):
        @pl.when(step == i)
        def _():
            copy.wait()

    panel_copies(wait)
    here = pl.ds(pl.multiple_of(step * tile, tile), tile)
    total = partial[...]
    for k in range(count):
        spot = slice(k * depth, (k + 1) * depth)
        total = total - product(panel[k, here, :], high[spot], low[spot])
    out[...] = total


def tie_kernel(x_ref, token_ref, out_ref):
    del x_ref, token_ref, out_ref


def tie(x, token):
    return pl.pallas_call(
        tie_kernel,
        out_shape=jax.ShapeDtypeStruct(x.shape, x.dtype),
        in_specs=[ANY, ANY],
        out_specs=ANY,
        input_output_aliases={0: 0},
        cost_estimate=TINY,
    )(x, token)


def struct(*shape, dtype=F32):
    return jax.ShapeDtypeStruct(shape, dtype)


def forward_substitution(diag_block, z_panel, mate):
    rows = lax.axis_size("row")
    levels = rows // 2
    last = levels - 1
    cols = lax.axis_size("col")
    size, full = diag_block.shape
    wide = z_panel.shape[1]
    width, half_wide, strip = 2 * size, wide // 2, size // 2
    dma = pltpu.SemaphoreType.DMA

    swap = [(i, i ^ 1) for i in range(rows)]
    cores = [(i, i ^ 1) for i in range(cols)]

    def move(x, source, target):
        return lax.ppermute(x, "row", [(2 * source + y, 2 * target + y) for y in (0, 1)])

    def strips(distances, *tokens):
        return pl.pallas_call(
            lambda *refs: strips_kernel(distances, *refs),
            out_shape=struct(strip, width * len(distances)),
            in_specs=[ANY] * (1 + len(tokens)),
            out_specs=VMEM,
            scratch_shapes=[dma((len(distances),))],
            compiler_params=params(),
            cost_estimate=TINY,
        )(diag_block, *tokens)

    z_own, z_send, corner = pl.pallas_call(
        stage_kernel,
        out_shape=(struct(half_wide, size), struct(half_wide, size), struct(size, size)),
        in_specs=[ANY, ANY],
        out_specs=(VMEM, VMEM, VMEM),
        scratch_shapes=[pltpu.VMEM((size, wide), F32), dma((2,))],
        compiler_params=params(),
        cost_estimate=TINY,
    )(z_panel, diag_block)
    z_other = lax.ppermute(z_send, "row", swap)
    corner_other = lax.ppermute(corner, "row", [p for p in swap if p[0] % 2 == 1])
    inv = pl.pallas_call(
        inverse_kernel,
        out_shape=struct(size, size),
        in_specs=[ANY, ANY],
        out_specs=VMEM,
        scratch_shapes=[pltpu.VMEM((size, size), F32), dma((1,))],
        compiler_params=params(),
        cost_estimate=TINY,
    )(diag_block, z_send)
    inv_other = lax.ppermute(inv, "row", swap)
    near_a = lax.ppermute(
        strips([1], mate), "row", [p for p in swap if p[0] >= 2])

    def solve(turn, came, strip_pairs, token, n_out=1):
        args = [z_own, z_other, inv, inv_other, corner, corner_other, diag_block]
        args += [*came, *strip_pairs]
        args += token
        deep = max(turn, 1) * width
        return pl.pallas_call(
            lambda *refs: solve_kernel(turn, len(args), *refs),
            out_shape=[struct(half_wide // n_out, width)] * n_out,
            in_specs=[ANY] * len(args),
            out_specs=[VMEM] * n_out,
            scratch_shapes=[
                pltpu.VMEM((2, half_wide, size), F32),
                pltpu.VMEM((3, size, size), F32),
                pltpu.VMEM((size, deep), F32),
                pltpu.VMEM((size, deep), F32),
                pltpu.VMEM((half_wide, deep), F32),
                dma((6 + 3 * turn,)),
            ],
            compiler_params=params(),
            cost_estimate=TINY,
        )(*args)

    def pick(sources, *tokens):
        args = [sources[z] for z in range(levels)]
        return pl.pallas_call(
            lambda *refs: pick_kernel(levels, *refs),
            out_shape=struct(*args[0].shape),
            in_specs=[ANY] * (levels + len(tokens)),
            out_specs=VMEM,
            scratch_shapes=[dma((1,))],
            compiler_params=params(8 * 1024 * 1024),
            cost_estimate=TINY,
        )(*args, *tokens)

    held, pieces = {}, {}
    strip_pairs = ()
    token = []

    def share(level, index, tokens):
        mine = pick(pieces[level][index], *tokens)
        return mine, lax.ppermute(mine, "row", swap)

    for turn in range(levels):
        came = [held[turn - d][turn] for d in range(1, turn + 1)]
        for k in range(turn):
            if turn < last:
                held[k][turn + 1] = move(held[k][turn], turn, turn + 1)
        own = solve(turn, came, strip_pairs, token, RETURNS if turn == last else 1)
        token = [own[0]]
        if turn < last:
            held[turn] = {turn: own[0], turn + 1: move(own[0], turn, turn + 1)}
        pieces[turn] = []
        for part in own:
            place = {turn: part}
            if turn < last:
                for z in range(turn - 1, -1, -1):
                    place[z] = move(place[z + 1], z + 1, z)
            pieces[turn].append(place)
        if turn == 0:
            strip_pairs = (near_a, lax.ppermute(tie(near_a, own[0]), "col", cores))
            far_a = lax.ppermute(
                strips(list(range(2, levels)), own[0]), "row", [p for p in swap if p[0] >= 4])
            far_b = lax.ppermute(far_a, "col", cores)
        if turn == 1:
            strip_pairs += (far_a, far_b)
        if turn == last - 1:
            for k in range(last - 1):
                pieces[k][0].update(held[k])
                shared = share(k, 0, token)
                pieces[k] = [shared]
                token = [shared[0]]
            token.append(pieces[0][0][1])
    for z in range(last - 1, -1, -1):
        for place in pieces[last]:
            place[z] = move(place[z + 1], z + 1, z)
    pieces[last - 1][0].update(held[last - 1])
    token.append(pieces[last - 2][0][1])
    shared = share(last - 1, 0, token)
    pieces[last - 1] = [shared]
    return pieces, share, own[0], shared[1]


def shards(diag_block, z_panel, panel_below, z_trail, norm_sq):
    cols = lax.axis_size("col")
    levels = lax.axis_size("row") // 2
    last = levels - 1
    rows, wide = z_trail.shape
    width = 2 * diag_block.shape[0]
    tile = min(512, rows)
    depth = panel_below.shape[1]
    dma = pltpu.SemaphoreType.DMA

    def flipped(x, flip):
        return lax.ppermute(x, "col", [(i, i ^ flip) for i in range(cols)])

    crossed = {flip: flipped(panel_below, flip) for flip in range(2, cols, 2)}
    panels = {0: panel_below, 1: flipped(panel_below, 1)}
    pieces, share, hold, token = forward_substitution(diag_block, z_panel, panels[1])
    for flip, x in crossed.items():
        panels[flip] = tie(x, hold)
        panels[flip ^ 1] = flipped(panels[flip], 1)
    flips = list(panels)
    slabs = [panels[flip] for flip in flips]

    def update(wanted, norm, out):
        plan, args = [], []
        for place, level in enumerate(wanted):
            line = 0
            for pair in pieces[level]:
                plan.append((level, place, line))
                args += pair
                line += pair[0].shape[0]
        first = out is z_trail
        span = width * len(wanted)
        aliases = {} if first else {len(args) + 1: 1}
        args += [norm, out, *slabs]
        line = pl.BlockSpec((1, wide), lambda i: (0, 0))
        whole = pl.BlockSpec((tile, wide), lambda i: (i, 0))
        return pl.pallas_call(
            lambda *refs: update_kernel(plan, flips, tile, len(args), *refs),
            grid=(rows // tile,),
            out_shape=(struct(1, wide), struct(rows, wide)),
            in_specs=[ANY] * (2 * len(plan)) + [line, whole] + [ANY] * len(slabs),
            out_specs=(line, whole),
            scratch_shapes=[
                pltpu.VMEM((wide, span), F32),
                pltpu.VMEM((span, wide), BF16),
                pltpu.VMEM((span, wide), BF16),
                pltpu.VMEM((span // depth, rows, depth), F32),
                dma((2 * len(plan),)),
                dma((rows // tile, span // depth)),
            ],
            input_output_aliases=aliases,
            compiler_params=params(30 * 1024 * 1024),
            cost_estimate=TINY,
        )(*args)

    pairs = []
    for index in range(RETURNS):
        pairs.append(share(last, index, [token]))
        token = pairs[-1][0]
    pieces[last] = pairs
    norm, out = update(range(last), norm_sq.reshape(1, wide), z_trail)
    norm, out = update([last], norm, out)
    return (norm.reshape(wide), out)


def solution(mesh):
    return jax.shard_map(
        shards,
        mesh=mesh,
        in_specs=(P("row", None), P("row", "col"), P("row", "col"), P("row", "col"), P("col")),
        out_specs=(P("col"), P("row", "col")),
        check_vma=False,
    )
```

```python
import jax
import jax.numpy as jnp
from jax import lax
from jax.experimental import pallas as pl
from jax.experimental.pallas import tpu as pltpu
from jax.sharding import PartitionSpec as P

F32 = jnp.float32
BF16 = jnp.bfloat16
HIGHEST = lax.Precision.HIGHEST
ANY = pl.BlockSpec(memory_space=pl.ANY)
VMEM = pl.BlockSpec(memory_space=pltpu.VMEM)
LIMIT = 62 * 1024 * 1024
RETURNS = 2
TINY = pl.CostEstimate(flops=1, bytes_accessed=1, transcendentals=0)


def params(limit=LIMIT):
    return pltpu.CompilerParams(vmem_limit_bytes=limit)


def mul(a, b):
    return jnp.dot(a, b, precision=HIGHEST, preferred_element_type=F32)


def mul_t(a, b):
    return lax.dot_general(
        a, b, (((1,), (1,)), ((), ())), precision=HIGHEST, preferred_element_type=F32
    )


def level_and_half():
    own_row = lax.axis_index("row")
    return own_row // 2, own_row % 2


def run_copies(pairs, sems):
    copies = [pltpu.make_async_copy(s, d, sems.at[i]) for i, (s, d) in enumerate(pairs)]
    for copy in copies:
        copy.start()
    for copy in copies:
        copy.wait()


def stage_kernel(z_ref, diag_ref, own_ref, send_ref, corner_ref, panel, sems):
    level, half = level_and_half()
    size = z_ref.shape[0]
    start = pl.multiple_of(level * 2 * size, 2 * size)
    run_copies([(z_ref, panel), (diag_ref.at[:, pl.ds(start, size)], corner_ref)], sems)
    width = z_ref.shape[1] // 2
    flipped = panel[...].T
    low, high = flipped[:width], flipped[width:]
    own_ref[...] = jnp.where(half == 0, low, high)
    send_ref[...] = jnp.where(half == 0, high, low)


def mul_n3(a, b):
    a_high, b_high = a.astype(BF16), b.astype(BF16)
    a_low = (a - a_high.astype(F32)).astype(BF16)
    b_low = (b - b_high.astype(F32)).astype(BF16)

    def dot(x, y):
        return jnp.dot(x, y, preferred_element_type=F32)

    return dot(a_high, b_high) + dot(a_high, b_low) + dot(a_low, b_high)


def inverse_of(tri):
    size = tri.shape[0]
    base = 16
    count = size // base
    rows = lax.broadcasted_iota(jnp.int32, (size, size), 0)
    cols = lax.broadcasted_iota(jnp.int32, (size, size), 1)
    same = (rows // base) == (cols // base)
    folded = jnp.sum(jnp.where(same, tri, 0.0).reshape(count, base, size), axis=0)
    lane = lax.broadcasted_iota(jnp.int32, (base, size), 1) % base
    line = lax.broadcasted_iota(jnp.int32, (base, size), 0)
    spread = jnp.concatenate([jnp.where(lane == k, folded, 0.0) for k in range(base)], axis=0)
    spread = mul(spread, jnp.where(same, 1.0, 0.0))
    rest = jnp.where(lane == line, 1.0, 0.0)
    done = jnp.zeros((base, size), F32)
    for k in range(base):
        column = spread[k * base:(k + 1) * base]
        solved = rest[k:k + 1] / column[k:k + 1]
        done = jnp.where(line == k, solved, done)
        rest = rest - jnp.where(line > k, column, 0.0) * solved
    full = jnp.where(same, jnp.concatenate([done] * count, axis=0), 0.0)
    step = base
    while step < size:
        pair = (rows // (2 * step)) == (cols // (2 * step))
        below = ((rows // step) % 2 == 1) & ((cols // step) % 2 == 0)
        off = jnp.where(pair & below, tri, 0.0)
        full = full - mul_n3(full, mul_n3(off, full))
        step *= 2
    return full


def inverse_kernel(diag_ref, token_ref, inv_ref, tile_ref, sems):
    del token_ref
    own_row = lax.axis_index("row")
    size = tile_ref.shape[0]
    source = diag_ref.at[:, pl.ds(pl.multiple_of(own_row * size, size), size)]
    run_copies([(source, tile_ref)], sems)
    inv_ref[...] = inverse_of(tile_ref[...])


def strips_kernel(distances, diag_ref, *refs):
    out_ref, sems = refs[-2:]
    level, _ = level_and_half()
    strip = out_ref.shape[0]
    width = 4 * strip
    core = lax.axis_index("col") % 2
    lines = pl.ds(pl.multiple_of(core * strip, strip), strip)
    pairs = []
    for slot, d in enumerate(distances):
        block = jnp.maximum(level - d, 0)
        source = diag_ref.at[lines, pl.ds(pl.multiple_of(block * width, width), width)]
        pairs.append((source, out_ref.at[:, pl.ds(slot * width, width)]))
    run_copies(pairs, sems)


def mul_t3(a, b):
    def parts(x):
        coarse = x.astype(BF16)
        return coarse, (x - coarse.astype(F32)).astype(BF16)

    def dot(x, y):
        return lax.dot_general(x, y, (((1,), (1,)), ((), ())), preferred_element_type=F32)

    (a_high, a_low), (b_high, b_low) = parts(a), parts(b)
    return dot(a_high, b_high) + dot(a_high, b_low) + dot(a_low, b_high)


def solve_kernel(turn, n_refs, *refs):
    z_own, z_other, inv_own, inv_other, corner_own, corner_other, diag, *rest_refs = refs[:n_refs]
    came = rest_refs[:turn]
    strips = rest_refs[turn:turn + 2 * min(turn, 2)]
    outs = refs[n_refs:-6]
    rest, tiles, low, low_other, earlier, sems = refs[-6:]
    level, half = level_and_half()
    core = lax.axis_index("col") % 2
    lines, size = rest.shape[1:]
    width = 2 * size
    strip = size // 2

    @pl.when(level == turn)
    def _():
        pairs = [
            (z_own, rest.at[0]),
            (z_other, rest.at[1]),
            (inv_own, tiles.at[0]),
            (inv_other, tiles.at[1]),
        ]
        here = pl.ds(pl.multiple_of(core * strip, strip), strip)
        there = pl.ds(pl.multiple_of((1 - core) * strip, strip), strip)
        if turn:
            pairs.append((diag.at[:, pl.ds(0, turn * width)], low))
        for d in range(1, turn + 1):
            spot = pl.ds((turn - d) * width, width)
            pairs.append((came[d - 1], earlier.at[:, spot]))
            for side, place in zip(strips[:2] if d == 1 else strips[2:], (here, there)):
                if d > 1:
                    side = side.at[:, pl.ds((d - 2) * width, width)]
                pairs.append((side, low_other.at[place, spot]))
        copies = [pltpu.make_async_copy(s, t, sems.at[i + 1]) for i, (s, t) in enumerate(pairs)]
        own_corner = pltpu.make_async_copy(corner_own, tiles.at[2], sems.at[0])
        other_corner = pltpu.make_async_copy(corner_other, tiles.at[2], sems.at[0])
        for copy in copies:
            copy.start()

        @pl.when(half == 1)
        def _():
            own_corner.start()

        @pl.when(half == 0)
        def _():
            other_corner.start()

        for copy in copies:
            copy.wait()
        own_corner.wait()
        first, second = rest[0], rest[1]
        if turn:
            first = first - mul_t3(earlier[...], low[...])
            second = second - mul_t3(earlier[...], low_other[...])
        upper = half == 0
        top = mul_t(jnp.where(upper, first, second), jnp.where(upper, tiles[0], tiles[1]))
        bottom = jnp.where(upper, second, first) - mul_t(top, tiles[2])
        bottom = mul_t(bottom, jnp.where(upper, tiles[1], tiles[0]))
        part = outs[0].shape[0]
        for q, out in enumerate(outs):
            out[:, :size] = top[q * part:(q + 1) * part]
            out[:, size:] = bottom[q * part:(q + 1) * part]


def pick_kernel(levels, *refs):
    out, sems = refs[-2:]
    level, _ = level_and_half()
    for z in range(levels):
        @pl.when(level == z)
        def _(z=z):
            run_copies([(refs[z], out)], sems)


def product(value, high, low):
    coarse = value.astype(BF16)
    fine = (value - coarse.astype(F32)).astype(BF16)
    total = jnp.dot(coarse, high, preferred_element_type=F32)
    total += jnp.dot(coarse, low, preferred_element_type=F32)
    return total + jnp.dot(fine, high, preferred_element_type=F32)


def update_kernel(plan, flips, tile, n_refs, *refs):
    ins = refs[:2 * len(plan)]
    norm, partial = refs[2 * len(plan):2 * len(plan) + 2]
    parts = refs[2 * len(plan) + 2:2 * len(plan) + 2 + len(flips)]
    norm_out, out, lines, high, low, panel, sems, panel_sems = refs[n_refs:]
    own_col = lax.axis_index("col")
    _, half = level_and_half()
    step = pl.program_id(0)
    rows, depth = parts[0].shape
    tiles = rows // tile
    wide, span = lines.shape
    width = span // len({level for level, _, _ in plan})
    count = span // depth
    first = min(level for level, _, _ in plan) * (width // depth)

    def panel_copies(act):
        for flip, part in zip(flips, parts):
            slot = lax.bitwise_xor(own_col, flip) - first

            @pl.when((slot >= 0) & (slot < count))
            def _(part=part, slot=slot):
                for i in range(tiles):
                    spot = pl.ds(i * tile, tile)
                    act(i, pltpu.make_async_copy(
                        part.at[spot], panel.at[slot, spot], panel_sems.at[i, slot]))

    @pl.when(step == 0)
    def _():
        pairs = []
        for index, (_, place, line) in enumerate(plan):
            for side in (0, 1):
                ref = ins[2 * index + side]
                number = ref.shape[0]
                start = jnp.where(half == side, 0, wide // 2) + line
                pairs.append((ref, lines.at[
                    pl.ds(pl.multiple_of(start, number), number), pl.ds(place * width, width)]))
        copies = [pltpu.make_async_copy(s, t, sems.at[i]) for i, (s, t) in enumerate(pairs)]
        for copy in copies:
            copy.start()
        panel_copies(lambda i, copy: copy.start())
        for copy in copies:
            copy.wait()
        total = norm[...]
        for k in range(span // width):
            block = lines[:, k * width:(k + 1) * width].T
            coarse = block.astype(BF16)
            high[k * width:(k + 1) * width] = coarse
            low[k * width:(k + 1) * width] = (block - coarse.astype(F32)).astype(BF16)
            total = total + jnp.sum(block * block, axis=0, keepdims=True)
        norm_out[...] = total

    def wait(i, copy):
        @pl.when(step == i)
        def _():
            copy.wait()

    panel_copies(wait)
    here = pl.ds(pl.multiple_of(step * tile, tile), tile)
    total = partial[...]
    for k in range(count):
        spot = slice(k * depth, (k + 1) * depth)
        total = total - product(panel[k, here, :], high[spot], low[spot])
    out[...] = total


def tie_kernel(x_ref, token_ref, out_ref):
    del x_ref, token_ref, out_ref


def tie(x, token):
    return pl.pallas_call(
        tie_kernel,
        out_shape=jax.ShapeDtypeStruct(x.shape, x.dtype),
        in_specs=[ANY, ANY],
        out_specs=ANY,
        input_output_aliases={0: 0},
        cost_estimate=TINY,
    )(x, token)


def struct(*shape, dtype=F32):
    return jax.ShapeDtypeStruct(shape, dtype)


def forward_substitution(diag_block, z_panel, mate):
    rows = lax.axis_size("row")
    levels = rows // 2
    last = levels - 1
    cols = lax.axis_size("col")
    size, full = diag_block.shape
    wide = z_panel.shape[1]
    width, half_wide, strip = 2 * size, wide // 2, size // 2
    dma = pltpu.SemaphoreType.DMA

    swap = [(i, i ^ 1) for i in range(rows)]
    cores = [(i, i ^ 1) for i in range(cols)]

    def move(x, source, target):
        return lax.ppermute(x, "row", [(2 * source + y, 2 * target + y) for y in (0, 1)])

    def strips(distances, *tokens):
        return pl.pallas_call(
            lambda *refs: strips_kernel(distances, *refs),
            out_shape=struct(strip, width * len(distances)),
            in_specs=[ANY] * (1 + len(tokens)),
            out_specs=VMEM,
            scratch_shapes=[dma((len(distances),))],
            compiler_params=params(),
            cost_estimate=TINY,
        )(diag_block, *tokens)

    z_own, z_send, corner = pl.pallas_call(
        stage_kernel,
        out_shape=(struct(half_wide, size), struct(half_wide, size), struct(size, size)),
        in_specs=[ANY, ANY],
        out_specs=(VMEM, VMEM, VMEM),
        scratch_shapes=[pltpu.VMEM((size, wide), F32), dma((2,))],
        compiler_params=params(),
        cost_estimate=TINY,
    )(z_panel, diag_block)
    z_other = lax.ppermute(z_send, "row", swap)
    corner_other = lax.ppermute(corner, "row", [p for p in swap if p[0] % 2 == 1])
    inv = pl.pallas_call(
        inverse_kernel,
        out_shape=struct(size, size),
        in_specs=[ANY, ANY],
        out_specs=VMEM,
        scratch_shapes=[pltpu.VMEM((size, size), F32), dma((1,))],
        compiler_params=params(),
        cost_estimate=TINY,
    )(diag_block, z_send)
    inv_other = lax.ppermute(inv, "row", swap)
    near_a = lax.ppermute(
        strips([1], mate), "row", [p for p in swap if p[0] >= 2])

    def solve(turn, came, strip_pairs, token, n_out=1):
        args = [z_own, z_other, inv, inv_other, corner, corner_other, diag_block]
        args += [*came, *strip_pairs]
        args += token
        deep = max(turn, 1) * width
        return pl.pallas_call(
            lambda *refs: solve_kernel(turn, len(args), *refs),
            out_shape=[struct(half_wide // n_out, width)] * n_out,
            in_specs=[ANY] * len(args),
            out_specs=[VMEM] * n_out,
            scratch_shapes=[
                pltpu.VMEM((2, half_wide, size), F32),
                pltpu.VMEM((3, size, size), F32),
                pltpu.VMEM((size, deep), F32),
                pltpu.VMEM((size, deep), F32),
                pltpu.VMEM((half_wide, deep), F32),
                dma((6 + 3 * turn,)),
            ],
            compiler_params=params(),
            cost_estimate=TINY,
        )(*args)

    def pick(sources, *tokens):
        args = [sources[z] for z in range(levels)]
        return pl.pallas_call(
            lambda *refs: pick_kernel(levels, *refs),
            out_shape=struct(*args[0].shape),
            in_specs=[ANY] * (levels + len(tokens)),
            out_specs=VMEM,
            scratch_shapes=[dma((1,))],
            compiler_params=params(8 * 1024 * 1024),
            cost_estimate=TINY,
        )(*args, *tokens)

    held, pieces = {}, {}
    strip_pairs = ()
    token = []

    def share(level, index, tokens):
        mine = pick(pieces[level][index], *tokens)
        return mine, lax.ppermute(mine, "row", swap)

    for turn in range(levels):
        came = [held[turn - d][turn] for d in range(1, turn + 1)]
        for k in range(turn):
            if turn < last:
                held[k][turn + 1] = move(held[k][turn], turn, turn + 1)
        own = solve(turn, came, strip_pairs, token, RETURNS if turn == last else 1)
        token = [own[0]]
        if turn < last:
            held[turn] = {turn: own[0], turn + 1: move(own[0], turn, turn + 1)}
        pieces[turn] = []
        for part in own:
            place = {turn: part}
            if turn < last:
                for z in range(turn - 1, -1, -1):
                    place[z] = move(place[z + 1], z + 1, z)
            pieces[turn].append(place)
        if turn == 0:
            strip_pairs = (near_a, lax.ppermute(tie(near_a, own[0]), "col", cores))
            far_a = lax.ppermute(
                strips(list(range(2, levels)), own[0]), "row", [p for p in swap if p[0] >= 4])
            far_b = lax.ppermute(far_a, "col", cores)
        if turn == 1:
            strip_pairs += (far_a, far_b)
        if turn == last - 1:
            for k in range(last - 1):
                pieces[k][0].update(held[k])
                shared = share(k, 0, token)
                pieces[k] = [shared]
                token = [shared[0]]
            token.append(pieces[0][0][1])
    for z in range(last - 1, -1, -1):
        for place in pieces[last]:
            place[z] = move(place[z + 1], z + 1, z)
    pieces[last - 1][0].update(held[last - 1])
    token.append(pieces[last - 2][0][1])
    shared = share(last - 1, 0, token)
    pieces[last - 1] = [shared]
    return pieces, share, own[0], shared[1]


def shards(diag_block, z_panel, panel_below, z_trail, norm_sq):
    cols = lax.axis_size("col")
    levels = lax.axis_size("row") // 2
    last = levels - 1
    rows, wide = z_trail.shape
    width = 2 * diag_block.shape[0]
    tile = min(1024, rows)
    depth = panel_below.shape[1]
    dma = pltpu.SemaphoreType.DMA

    def flipped(x, flip):
        return lax.ppermute(x, "col", [(i, i ^ flip) for i in range(cols)])

    crossed = {flip: flipped(panel_below, flip) for flip in range(2, cols, 2)}
    panels = {0: panel_below, 1: flipped(panel_below, 1)}
    pieces, share, hold, token = forward_substitution(diag_block, z_panel, panels[1])
    for flip, x in crossed.items():
        panels[flip] = tie(x, hold)
        panels[flip ^ 1] = flipped(panels[flip], 1)
    flips = list(panels)
    slabs = [panels[flip] for flip in flips]

    def update(wanted, norm, out):
        plan, args = [], []
        for place, level in enumerate(wanted):
            line = 0
            for pair in pieces[level]:
                plan.append((level, place, line))
                args += pair
                line += pair[0].shape[0]
        first = out is z_trail
        span = width * len(wanted)
        aliases = {} if first else {len(args) + 1: 1}
        args += [norm, out, *slabs]
        line = pl.BlockSpec((1, wide), lambda i: (0, 0))
        whole = pl.BlockSpec((tile, wide), lambda i: (i, 0))
        return pl.pallas_call(
            lambda *refs: update_kernel(plan, flips, tile, len(args), *refs),
            grid=(rows // tile,),
            out_shape=(struct(1, wide), struct(rows, wide)),
            in_specs=[ANY] * (2 * len(plan)) + [line, whole] + [ANY] * len(slabs),
            out_specs=(line, whole),
            scratch_shapes=[
                pltpu.VMEM((wide, span), F32),
                pltpu.VMEM((span, wide), BF16),
                pltpu.VMEM((span, wide), BF16),
                pltpu.VMEM((span // depth, rows, depth), F32),
                dma((2 * len(plan),)),
                dma((rows // tile, span // depth)),
            ],
            input_output_aliases=aliases,
            compiler_params=params(30 * 1024 * 1024),
            cost_estimate=TINY,
        )(*args)

    pairs = []
    for index in range(RETURNS):
        pairs.append(share(last, index, [token]))
        token = pairs[-1][0]
    pieces[last] = pairs
    norm, out = update(range(last), norm_sq.reshape(1, wide), z_trail)
    norm, out = update([last], norm, out)
    return (norm.reshape(wide), out)


def solution(mesh):
    return jax.shard_map(
        shards,
        mesh=mesh,
        in_specs=(P("row", None), P("row", "col"), P("row", "col"), P("row", "col"), P("col")),
        out_specs=(P("col"), P("row", "col")),
        check_vma=False,
    )
```
